32 devices in a mesh: dp: 8 (over y, x, core), mp: 4 (over z).
Axes of the slice: x: 2, y: 2, z: 4, core: 2. Of those that a mesh axis runs over, the one named last changes fastest.
Arguments:
- acts: bfloat16 [1024, 8192], P('dp', 'mp'), may hold values from -6 to 6
- grads: bfloat16 [1024, 28672], P('dp', 'mp'), may hold values from -6 to 6
- proj_in: bfloat16 [8192, 64], replicated, may hold values from -0.0625 to 0.0625
- block_vals: bfloat16 [128, 128, 64], replicated, may hold values from -0.046875 to 0.046875
- block_index: int32 [128], replicated, may hold values from 0 to 223, as said below
- assign: int32 [8, 128], P('dp'), may hold values from 0 to 127, each once within a row
Outputs:
- features: bfloat16 [1024, 4096], P(('dp', 'mp'))
- factor: float32 [8, 512, 512], P('mp')
The draws below stay inside these ranges and needn't reach their ends.
Inputs may be any that keep to these rules, and one draw needn't show every extreme that they name: `block_index`: 128 distinct row blocks. Each row of assign names every example of its group once.
All inputs are finite; a program needn't handle non-finite values.
Results may differ from the reference program's by a relative error of at most 0.013.
Values may be sent and summed in bfloat16 or wider, within the bound.
A program may use at most 64 MiB of HBM per device.

```python
import jax
import jax.numpy as jnp
from jax import lax

D = 8192
FF = 28672
K_IN = 64
K_OUT = 64
BLK = 128
NBLK = 128
FB = 512
FEAT = 4096
NBLOCKS = 224
E_DP = 128
GROUPS = 8
EXAMPLES = 1024


def draw_block_index(key, part):
    return jax.random.permutation(key, FF // BLK)[:NBLK].astype(jnp.int32)


def levels(stream_key, shape, split, least, high):
    factor_of, own = 1.0, jax.random.fold_in(stream_key, 6)
    for axis_at, blocks in split:
        steps = jnp.exp(jax.random.uniform(jax.random.fold_in(own, axis_at), (blocks,), jnp.float32, least / len(split), high / len(split)))
        factor_of = factor_of * jnp.repeat(steps, shape[axis_at] // blocks).reshape([-1 if axis == axis_at else 1 for axis in range(len(shape))])
    return factor_of


def scatter_about(key, dims, scale, most, split=(), kind=jnp.bfloat16):
    entries = scale * jax.random.normal(key, dims, jnp.float32)
    if split:
        entries = entries * levels(key, dims, split, -0.22, 0.18)
    return jnp.clip(entries, -most, most).astype(kind)


def setup_inputs(seed: int = 0) -> dict:
    splits = jax.random.split(jax.random.key(seed), 7)
    return {
        "acts": scatter_about(splits[0], (EXAMPLES, D), 1.0, 6.0, ((0, 8), (1, 4))),
        "grads": scatter_about(splits[1], (EXAMPLES, FF), 1.0, 6.0, ((0, 8), (1, 4))),
        "proj_in": scatter_about(splits[2], (D, K_IN), D ** -0.5, 0.0625),
        "block_vals": scatter_about(splits[3], (NBLK, BLK, K_OUT), (NBLK * BLK) ** -0.5, 0.046875),
        "block_index": draw_block_index(jax.random.fold_in(splits[6], 71), 0),
        "assign": jax.vmap(lambda own: jax.random.permutation(own, E_DP))(jax.random.split(splits[5], GROUPS)).reshape((GROUPS, E_DP)).astype(jnp.int32),
    }


def reference(acts, grads, proj_in, block_vals, block_index, assign):

    def one_group(group):
        rows = assign[group].astype(jnp.int32) + (group * E_DP).astype(jnp.int32)
        ordered_acts = jnp.take(acts, rows, axis=0)
        ordered_grads = jnp.take(grads, rows, axis=0)
        in_coords = jnp.dot(ordered_acts.astype(jnp.float32), proj_in.astype(jnp.float32), preferred_element_type=jnp.float32).astype(jnp.bfloat16)
        grid = ordered_grads.reshape(E_DP, NBLOCKS, BLK)
        picked = jnp.take(grid, block_index, axis=1)
        out_coords = jnp.einsum('rtk,tko->ro', picked.astype(jnp.float32), block_vals.astype(jnp.float32)).astype(jnp.bfloat16)
        outer = in_coords.astype(jnp.float32)[:, :, None] * out_coords.astype(jnp.float32)[:, None, :]
        return outer.reshape(E_DP, FEAT).astype(jnp.bfloat16)
    features = lax.map(one_group, jnp.arange(GROUPS, dtype=jnp.int32)).reshape(EXAMPLES, FEAT)

    def one_block(block):
        columns = lax.dynamic_slice_in_dim(features, (block * FB).astype(jnp.int32), FB, 1)
        return jnp.dot(columns.T.astype(jnp.float32), columns.astype(jnp.float32), preferred_element_type=jnp.float32)
    gram = lax.map(one_block, jnp.arange(FEAT // FB, dtype=jnp.int32))
    identity = jnp.eye(FB, dtype=jnp.float32)
    covariance = gram / EXAMPLES + 0.05 * identity
    lower = jnp.linalg.cholesky(covariance)
    factor = jnp.swapaxes(lower, 1, 2)
    return (features, factor)
```

```python
import functools

import jax
import jax.numpy as jnp
from jax import lax
from jax.experimental import pallas as pl
from jax.experimental.pallas import tpu as pltpu
from jax.sharding import PartitionSpec as P

MESH = pl.DeviceIdType.MESH
FB = 512
DAMPING = 0.05
TILE = 128
STEP = 16
F32 = jnp.float32
BF16 = jnp.bfloat16


def dot_nt(a, b):
    return lax.dot_general(a, b, (((1,), (1,)), ((), ())), preferred_element_type=F32)


def dot_tn(a, b):
    return lax.dot_general(a, b, (((0,), (0,)), ((), ())), preferred_element_type=F32)


def project_kernel(index_ref, assign_ref, acts_ref, grads_ref, proj_ref, vals_ref, out_ref, dense):
    own = lax.axis_index("mp")
    width = acts_ref.shape[1]
    blk = vals_ref.shape[2]
    k_in = proj_ref.shape[0]
    local = grads_ref.shape[1] // blk
    dense[...] = jnp.zeros_like(dense)

    def place(t, carry):
        at = index_ref[t] - own * local
        at = jnp.where((at >= 0) & (at < local), at, local)
        dense[:, pl.ds(pl.multiple_of(at * blk, blk), blk)] = vals_ref[t]
        return carry

    lax.fori_loop(0, vals_ref.shape[0], place, 0, unroll=8)
    cols = pl.ds(pl.multiple_of(own * width, width), width)
    in_part = dot_nt(proj_ref[:, cols], acts_ref[...])
    out_part = dot_nt(dense[:, : local * blk], grads_ref[...])
    rows = acts_ref.shape[0]
    pick = (lax.broadcasted_iota(jnp.int32, (rows, rows), 0) == assign_ref[...]).astype(BF16)
    out_ref[:k_in] = jnp.dot(in_part.astype(BF16), pick, preferred_element_type=F32).astype(BF16)
    out_ref[k_in:] = jnp.dot(out_part.astype(BF16), pick, preferred_element_type=F32).astype(BF16)


def exchange_kernel(mp, dp, k_in, need, part_ref, full_ref, gath_ref, recv, slab, s1, r1, s2, r2):
    m = lax.axis_index("mp")
    d = lax.axis_index("dp")
    barrier = pltpu.get_barrier_semaphore()
    for o in range(1, mp):
        pl.semaphore_signal(barrier, inc=1, device_id=(d, lax.rem(m + o, mp)), device_id_type=MESH)
    for o in range(1, dp):
        pl.semaphore_signal(barrier, inc=1, device_id=(lax.rem(d + o, dp), m), device_id_type=MESH)
    pl.semaphore_wait(barrier, mp + dp - 2)
    copies = []
    for o in range(1, mp):
        copy = pltpu.make_async_remote_copy(
            src_ref=part_ref, dst_ref=recv.at[m], send_sem=s1.at[o - 1], recv_sem=r1.at[o - 1],
            device_id=(d, lax.rem(m + o, mp)), device_id_type=MESH)
        copy.start()
        copies.append(copy)
    recv[m] = part_ref[...]
    for copy in copies:
        copy.wait()
    total = recv[0].astype(F32)
    for j in range(1, mp):
        total = total + recv[j].astype(F32)
    full_ref[...] = total.astype(BF16)
    first = (m * (k_in // mp)) // need * need
    slab[:need] = full_ref[pl.ds(pl.multiple_of(first, need), need), :]
    slab[need:] = full_ref[k_in:, :]
    copies = []
    for o in range(1, dp):
        copy = pltpu.make_async_remote_copy(
            src_ref=slab, dst_ref=gath_ref.at[d], send_sem=s2.at[o - 1], recv_sem=r2.at[o - 1],
            device_id=(lax.rem(d + o, dp), m), device_id_type=MESH)
        copy.start()
        copies.append(copy)
    gath_ref[d] = slab[...]
    for copy in copies:
        copy.wait()


def split(x):
    high = x.astype(BF16).astype(F32)
    return high, x - high


def eliminate(cols, rows):
    sub = lax.broadcasted_iota(jnp.int32, (STEP, TILE), 0)
    scale = jnp.zeros((STEP, TILE), F32)
    for k in range(STEP):
        col = cols[k]
        root = lax.rsqrt(col[k:k + 1, :])
        inv = root * root
        scale = jnp.where(sub == k, root, scale)
        if k == STEP - 1:
            break
        below = jnp.where(sub > k, col, 0.0)
        for j in range(k + 1, STEP):
            cols[j] = cols[j] - (below * col[j:j + 1, :]) * inv
        below = below * inv
        for t in range(len(rows)):
            rows[t] = rows[t] - below * rows[t][k:k + 1, :]
    return [row * scale for row in rows]


def factor_kernel(mp, k_in, k_out, need, gath_ref, full_ref, feat_ref, factor_ref, ft, inf, cov, panel, upper):
    m = lax.axis_index("mp")
    dp, _, ex = gath_ref.shape
    nb = factor_ref.shape[0]
    tiles = FB // TILE
    per = FB // k_out
    skip = m * (k_in // mp) - (m * (k_in // mp)) // need * need

    mine = feat_ref.shape[0]
    pick = (lax.broadcasted_iota(jnp.int32, (mine, ex), 0) + m * mine
            == lax.broadcasted_iota(jnp.int32, (mine, ex), 1)).astype(BF16)
    coords = dot_nt(pick, full_ref[...])
    lane = lax.broadcasted_iota(jnp.int32, (mine, TILE), 1)
    outs = jnp.concatenate([coords[:, k_in:], coords[:, k_in:]], axis=1)
    for t in range(k_in // 2):
        left = jnp.broadcast_to(coords[:, 2 * t:2 * t + 1], (mine, TILE))
        right = jnp.broadcast_to(coords[:, 2 * t + 1:2 * t + 2], (mine, TILE))
        feat_ref[:, t * TILE:(t + 1) * TILE] = (jnp.where(lane < k_out, left, right) * outs).astype(BF16)

    def expand(g, carry):
        inf[...] = gath_ref[g, :need, :].astype(F32)
        out = gath_ref[g, need:, :].astype(F32)
        at = pl.ds(pl.multiple_of(g * ex, ex), ex)
        for p in range(nb * per):
            if nb * per == need:
                row = inf[p:p + 1, :]
            else:
                row = inf[pl.ds(skip + p, 1), :]
            ft[p * k_out:(p + 1) * k_out, at] = (row * out).astype(BF16)
        return carry

    lax.fori_loop(0, dp, expand, 0)

    total = dp * ex
    chunk = min(total, 1024)
    half = FB // 2
    diag = jnp.where(lax.broadcasted_iota(jnp.int32, (half, half), 0)
                     == lax.broadcasted_iota(jnp.int32, (half, half), 1), DAMPING, 0.0)
    for c in range(nb):
        for i in range(2):
            for j in range(i, 2):
                def piece(n):
                    at = pl.ds(pl.multiple_of(n * chunk, chunk), chunk)
                    return dot_nt(ft[c * FB + i * half:c * FB + (i + 1) * half, at],
                                  ft[c * FB + j * half:c * FB + (j + 1) * half, at])
                gram = piece(0)
                if total > chunk:
                    gram = lax.fori_loop(1, total // chunk, lambda n, acc: acc + piece(n), gram)
                gram = gram * (1.0 / total)
                if i == j:
                    gram = gram + diag
                cov[c, i * half:(i + 1) * half, j * half:(j + 1) * half] = gram

    def block_row(b, carry):
        at = pl.ds(pl.multiple_of(b * TILE, TILE), TILE)

        def tile_at(t):
            return pl.ds(pl.multiple_of(lax.rem(b + t, tiles) * TILE, TILE), TILE)

        for c in range(nb):
            for t in range(tiles):
                panel[c, t] = cov[c, at, tile_at(t)]
        for s in range(TILE // STEP):
            lo, hi = s * STEP, (s + 1) * STEP
            cols = []
            for c in range(nb):
                pivot = panel[c, 0, lo:hi, :]
                cols.append([jnp.broadcast_to(pivot[:, lo + j:lo + j + 1], (STEP, TILE)) for j in range(STEP)])
            for c in range(nb):
                rows = eliminate(cols[c], [panel[c, t, lo:hi, :] for t in range(tiles)])
                parts = [split(row) for row in rows]
                for t in range(tiles):
                    upper[c, t, lo:hi, :] = rows[t]
                if hi < TILE:
                    h, l = parts[0]
                    left = jnp.concatenate([h, h, l, l], axis=0)[:, hi:].astype(BF16)
                    right = jnp.concatenate(
                        [jnp.concatenate([h, l, h, l], axis=0) for h, l in parts], axis=1).astype(BF16)
                    update = dot_tn(left, right)
                    for t in range(tiles):
                        panel[c, t, hi:, :] = panel[c, t, hi:, :] - update[:, t * TILE:(t + 1) * TILE]
        tri = (lax.broadcasted_iota(jnp.int32, (TILE, TILE), 1)
               >= lax.broadcasted_iota(jnp.int32, (TILE, TILE), 0))
        for c in range(nb):
            factor_ref[c, at, tile_at(0)] = jnp.where(tri, upper[c, 0], 0.0)
            for t in range(1, tiles):
                factor_ref[c, at, tile_at(t)] = jnp.where(b + t < tiles, upper[c, t], 0.0)
        for i in range(1, tiles):
            @pl.when(b + i < tiles)
            def _():
                here = pl.ds(pl.multiple_of(lax.rem(b + i, tiles) * TILE, TILE), TILE)
                for c in range(nb):
                    h, l = split(upper[c, i])
                    left = jnp.concatenate([h, h, l, l], axis=0).astype(BF16)
                    for t in range(i, tiles):
                        h, l = split(upper[c, t])
                        right = jnp.concatenate([h, l, h, l], axis=0).astype(BF16)
                        cov[c, here, tile_at(t)] = cov[c, here, tile_at(t)] - dot_tn(left, right)
        return carry

    lax.fori_loop(0, tiles, block_row, 0)


def shards(acts, grads, proj_in, block_vals, block_index, assign):
    mp = lax.axis_size("mp")
    dp = lax.axis_size("dp")
    ex = acts.shape[0]
    k_in = proj_in.shape[1]
    nblk, blk, k_out = block_vals.shape
    feat = k_in * k_out
    nb = feat // FB // mp
    need = max(16, k_in // mp)
    vmem = pl.BlockSpec(memory_space=pltpu.VMEM)
    part = pl.pallas_call(
        project_kernel,
        out_shape=jax.ShapeDtypeStruct((k_in + k_out, ex), BF16),
        in_specs=[pl.BlockSpec(memory_space=pltpu.SMEM)] + [vmem] * 5,
        out_specs=vmem,
        scratch_shapes=[pltpu.VMEM((k_out, grads.shape[1] + blk), BF16)],
        compiler_params=pltpu.CompilerParams(vmem_limit_bytes=48 << 20),
    )(block_index, assign, acts, grads, proj_in.T, jnp.swapaxes(block_vals, 1, 2))
    full, gath = pl.pallas_call(
        functools.partial(exchange_kernel, mp, dp, k_in, need),
        out_shape=(jax.ShapeDtypeStruct((k_in + k_out, ex), BF16),
                   jax.ShapeDtypeStruct((dp, need + k_out, ex), BF16)),
        in_specs=[vmem],
        out_specs=(vmem, vmem),
        scratch_shapes=[
            pltpu.VMEM((mp, k_in + k_out, ex), BF16),
            pltpu.VMEM((need + k_out, ex), BF16),
            pltpu.SemaphoreType.DMA((mp - 1,)),
            pltpu.SemaphoreType.DMA((mp - 1,)),
            pltpu.SemaphoreType.DMA((dp - 1,)),
            pltpu.SemaphoreType.DMA((dp - 1,)),
        ],
        compiler_params=pltpu.CompilerParams(collective_id=0, has_side_effects=True),
    )(part)
    features, factor = pl.pallas_call(
        functools.partial(factor_kernel, mp, k_in, k_out, need),
        out_shape=(jax.ShapeDtypeStruct((ex // mp, feat), BF16),
                   jax.ShapeDtypeStruct((nb, FB, FB), F32)),
        in_specs=[vmem, vmem],
        out_specs=(vmem, vmem),
        scratch_shapes=[
            pltpu.VMEM((nb * FB, dp * ex), BF16),
            pltpu.VMEM((need, ex), F32),
            pltpu.VMEM((nb, FB, FB), F32),
            pltpu.VMEM((nb, FB // TILE, TILE, TILE), F32),
            pltpu.VMEM((nb, FB // TILE, TILE, TILE), F32),
        ],
        compiler_params=pltpu.CompilerParams(vmem_limit_bytes=48 << 20),
    )(gath, full)
    return features, factor


def solution(mesh):
    return jax.shard_map(
        shards,
        mesh=mesh,
        in_specs=(P("dp", "mp"), P("dp", "mp"), P(), P(), P(), P("dp", None)),
        out_specs=(P(("dp", "mp"), None), P("mp", None, None)),
        check_vma=False,
    )
```

```python
import functools

import jax
import jax.numpy as jnp
from jax import lax
from jax.experimental import pallas as pl
from jax.experimental.pallas import tpu as pltpu
from jax.sharding import PartitionSpec as P

MESH = pl.DeviceIdType.MESH
FB = 512
DAMPING = 0.05
TILE = 128
STEP = 16
F32 = jnp.float32
BF16 = jnp.bfloat16


def dot_nt(a, b):
    return lax.dot_general(a, b, (((1,), (1,)), ((), ())), preferred_element_type=F32)


def dot_tn(a, b):
    return lax.dot_general(a, b, (((0,), (0,)), ((), ())), preferred_element_type=F32)


def coords_kernel(mp, dp, need, inverse_ref, assign_ref, acts_hbm, grads_hbm, proj_hbm, vals_hbm, full_ref, gath_ref,
                  acts, grads, proj, vals, dense, part, recv, slab, ins, s1, r1, s2, r2):
    m = lax.axis_index("mp")
    d = lax.axis_index("dp")
    barrier = pltpu.get_barrier_semaphore()
    for o in range(1, mp):
        pl.semaphore_signal(barrier, inc=1, device_id=(d, lax.rem(m + o, mp)), device_id_type=MESH)
    for o in range(1, dp):
        pl.semaphore_signal(barrier, inc=1, device_id=(lax.rem(d + o, dp), m), device_id_type=MESH)
    ex, width = acts.shape
    k_in = proj.shape[0]
    nblk, k_out, blk = vals_hbm.shape
    local = grads.shape[1] // blk
    cols = pl.ds(pl.multiple_of(m * width, width), width)
    loads = [
        pltpu.make_async_copy(proj_hbm.at[:, cols], proj, ins.at[0]),
        pltpu.make_async_copy(acts_hbm, acts, ins.at[1]),
        pltpu.make_async_copy(vals_hbm, vals.at[pl.ds(0, nblk)], ins.at[2]),
        pltpu.make_async_copy(grads_hbm, grads, ins.at[3]),
    ]
    for load in loads:
        load.start()
    vals[nblk] = jnp.zeros((k_out, blk), BF16)
    pick = (lax.broadcasted_iota(jnp.int32, (ex, ex), 0) == assign_ref[...]).astype(BF16)

    def send(lo, hi, at):
        copies = []
        for o in range(1, mp):
            copy = pltpu.make_async_remote_copy(
                src_ref=part.at[pl.ds(lo, hi - lo)], dst_ref=recv.at[m, pl.ds(lo, hi - lo)],
                send_sem=s1.at[at, o - 1], recv_sem=r1.at[at, o - 1],
                device_id=(d, lax.rem(m + o, mp)), device_id_type=MESH)
            copy.start()
            copies.append(copy)
        recv[m, lo:hi] = part[lo:hi]
        return copies

    loads[0].wait()
    loads[1].wait()
    in_part = dot_nt(proj[...], acts[...])
    part[:k_in] = jnp.dot(in_part.astype(BF16), pick, preferred_element_type=F32).astype(BF16)
    pl.semaphore_wait(barrier, mp + dp - 2)
    in_copies = send(0, k_in, 0)
    loads[2].wait()
    for b in range(local):
        dense[:, b * blk:(b + 1) * blk] = vals[inverse_ref[b]]
    loads[3].wait()
    out_part = dot_nt(dense[...], grads[...])
    part[k_in:] = jnp.dot(out_part.astype(BF16), pick, preferred_element_type=F32).astype(BF16)
    out_copies = send(k_in, k_in + k_out, 1)

    def add_up(lo, hi):
        total = recv[0, lo:hi].astype(F32)
        for j in range(1, mp):
            total = total + recv[j, lo:hi].astype(F32)
        return total.astype(BF16)

    for copy in in_copies:
        copy.wait()
    full_ref[:k_in] = add_up(0, k_in)
    first = (m * (k_in // mp)) // need * need
    slab[:need] = full_ref[pl.ds(pl.multiple_of(first, need), need), :]
    for copy in out_copies:
        copy.wait()
    slab[need:] = add_up(k_in, k_in + k_out)
    copies = []
    for o in range(1, dp):
        copy = pltpu.make_async_remote_copy(
            src_ref=slab, dst_ref=gath_ref.at[d], send_sem=s2.at[o - 1], recv_sem=r2.at[o - 1],
            device_id=(lax.rem(d + o, dp), m), device_id_type=MESH)
        copy.start()
        copies.append(copy)
    full_ref[k_in:] = slab[need:]
    gath_ref[d] = slab[...]
    for copy in copies:
        copy.wait()


def split(x):
    high = x.astype(BF16).astype(F32)
    return high, x - high


def eliminate(heads, tails, rows):
    half = STEP // 2
    sub = lax.broadcasted_iota(jnp.int32, (half, TILE), 0)
    scale = [jnp.zeros((half, TILE), F32) for _ in range(2)]
    tops = [row[:half] for row in rows]
    ends = [row[half:] for row in rows]
    for k in range(STEP):
        low, at = k < half, k % half
        pivot = heads[k] if low else tails[k]
        root = jnp.broadcast_to(lax.rsqrt(pivot[at:at + 1, :]), (half, TILE))
        inv = root * root
        scale[k // half] = jnp.where(sub == at, root, scale[k // half])
        if k == STEP - 1:
            break
        end = tails[k] * inv
        if low:
            top = heads[k] * inv
            for j in range(k + 1, half):
                entry = heads[k][j:j + 1, :]
                heads[j] = heads[j] - top * entry
                tails[j] = tails[j] - end * entry
            for j in range(half, STEP):
                tails[j] = tails[j] - end * tails[k][j - half:j - half + 1, :]
            top = jnp.where(sub > at, top, 0.0)
            for t in range(len(rows)):
                row = tops[t][at:at + 1, :]
                if at < half - 1:
                    tops[t] = tops[t] - top * row
                ends[t] = ends[t] - end * row
        else:
            for j in range(k + 1, STEP):
                tails[j] = tails[j] - end * tails[k][j - half:j - half + 1, :]
            end = jnp.where(sub > at, end, 0.0)
            for t in range(len(rows)):
                ends[t] = ends[t] - end * ends[t][at:at + 1, :]
    return [jnp.concatenate([top * scale[0], end * scale[1]], axis=0) for top, end in zip(tops, ends)]


def factor_kernel(mp, k_in, k_out, need, gath_hbm, full_hbm, feat_hbm, factor_hbm,
                  gath_ref, full_ref, feat_ref, factor_ref, ft, inf, cov, panel, upper, ins, fsem, osem):
    m = lax.axis_index("mp")
    dp, _, ex = gath_ref.shape
    nb = factor_ref.shape[0]
    tiles = FB // TILE
    per = FB // k_out
    skip = m * (k_in // mp) - (m * (k_in // mp)) // need * need

    full_load = pltpu.make_async_copy(full_hbm, full_ref, ins.at[0])
    gath_load = pltpu.make_async_copy(gath_hbm, gath_ref, ins.at[1])
    full_load.start()
    gath_load.start()
    full_load.wait()

    mine = feat_ref.shape[0]
    pick = (lax.broadcasted_iota(jnp.int32, (mine, ex), 0) + m * mine
            == lax.broadcasted_iota(jnp.int32, (mine, ex), 1)).astype(BF16)
    coords = dot_nt(pick, full_ref[...])
    lane = lax.broadcasted_iota(jnp.int32, (mine, TILE), 1)
    outs = jnp.concatenate([coords[:, k_in:], coords[:, k_in:]], axis=1)
    for t in range(k_in // 2):
        left = jnp.broadcast_to(coords[:, 2 * t:2 * t + 1], (mine, TILE))
        right = jnp.broadcast_to(coords[:, 2 * t + 1:2 * t + 2], (mine, TILE))
        feat_ref[:, t * TILE:(t + 1) * TILE] = (jnp.where(lane < k_out, left, right) * outs).astype(BF16)

    feat_store = pltpu.make_async_copy(feat_ref, feat_hbm, fsem)
    feat_store.start()
    gath_load.wait()

    def expand(g, carry):
        inf[...] = gath_ref[g, :need, :].astype(F32)
        out = gath_ref[g, need:, :].astype(F32)
        at = pl.ds(pl.multiple_of(g * ex, ex), ex)
        for p in range(nb * per):
            if nb * per == need:
                row = inf[p:p + 1, :]
            else:
                row = inf[pl.ds(skip + p, 1), :]
            ft[p * k_out:(p + 1) * k_out, at] = (row * out).astype(BF16)
        return carry

    lax.fori_loop(0, dp, expand, 0)

    total = dp * ex
    chunk = min(total, 1024)
    half = FB // 2
    diag = jnp.where(lax.broadcasted_iota(jnp.int32, (half, half), 0)
                     == lax.broadcasted_iota(jnp.int32, (half, half), 1), DAMPING, 0.0)
    for c in range(nb):
        for i in range(2):
            for j in range(i, 2):
                def piece(n):
                    at = pl.ds(pl.multiple_of(n * chunk, chunk), chunk)
                    return dot_nt(ft[c * FB + i * half:c * FB + (i + 1) * half, at],
                                  ft[c * FB + j * half:c * FB + (j + 1) * half, at])
                gram = piece(0)
                if total > chunk:
                    gram = lax.fori_loop(1, total // chunk, lambda n, acc: acc + piece(n), gram)
                gram = gram * (1.0 / total)
                if i == j:
                    gram = gram + diag
                cov[c, i * half:(i + 1) * half, j * half:(j + 1) * half] = gram

    def block_row(b, carry):
        at = pl.ds(pl.multiple_of(b * TILE, TILE), TILE)

        def tile_at(t):
            return pl.ds(pl.multiple_of(lax.rem(b + t, tiles) * TILE, TILE), TILE)

        for c in range(nb):
            for t in range(tiles):
                panel[c, t] = cov[c, at, tile_at(t)]
        for s in range(TILE // STEP):
            lo, hi = s * STEP, (s + 1) * STEP
            cols = []
            for c in range(nb):
                pivot = panel[c, 0, lo:hi, :]
                half = STEP // 2
                cols.append((
                    [jnp.broadcast_to(pivot[:half, lo + j:lo + j + 1], (half, TILE)) for j in range(half)],
                    [jnp.broadcast_to(pivot[half:, lo + j:lo + j + 1], (half, TILE)) for j in range(STEP)]))
            for c in range(nb):
                rows = eliminate(*cols[c], [panel[c, t, lo:hi, :] for t in range(tiles)])
                parts = [split(row) for row in rows]
                for t in range(tiles):
                    upper[c, t, lo:hi, :] = rows[t]
                if hi < TILE:
                    h, l = parts[0]
                    left = jnp.concatenate([h, h, l, l], axis=0)[:, hi:].astype(BF16)
                    right = jnp.concatenate(
                        [jnp.concatenate([h, l, h, l], axis=0) for h, l in parts], axis=1).astype(BF16)
                    update = dot_tn(left, right)
                    for t in range(tiles):
                        panel[c, t, hi:, :] = panel[c, t, hi:, :] - update[:, t * TILE:(t + 1) * TILE]
        tri = (lax.broadcasted_iota(jnp.int32, (TILE, TILE), 1)
               >= lax.broadcasted_iota(jnp.int32, (TILE, TILE), 0))
        for c in range(nb):
            factor_ref[c, at, tile_at(0)] = jnp.where(tri, upper[c, 0], 0.0)
            for t in range(1, tiles):
                factor_ref[c, at, tile_at(t)] = jnp.where(b + t < tiles, upper[c, t], 0.0)
            pltpu.make_async_copy(factor_ref.at[c, at], factor_hbm.at[c, at], osem.at[c, b]).start()
        for i in range(1, tiles):
            @pl.when(b + i < tiles)
            def _():
                here = pl.ds(pl.multiple_of(lax.rem(b + i, tiles) * TILE, TILE), TILE)
                for c in range(nb):
                    h, l = split(upper[c, i])
                    left = jnp.concatenate([h, h, l, l], axis=0).astype(BF16)
                    for t in range(i, tiles):
                        h, l = split(upper[c, t])
                        right = jnp.concatenate([h, l, h, l], axis=0).astype(BF16)
                        cov[c, here, tile_at(t)] = cov[c, here, tile_at(t)] - dot_tn(left, right)
        return carry

    lax.fori_loop(0, tiles, block_row, 0)
    feat_store.wait()
    for c in range(nb):
        for b in range(tiles):
            at = pl.ds(b * TILE, TILE)
            pltpu.make_async_copy(factor_ref.at[c, at], factor_hbm.at[c, at], osem.at[c, b]).wait()


def shards(acts, grads, proj_in, block_vals, block_index, assign):
    mp = lax.axis_size("mp")
    dp = lax.axis_size("dp")
    ex = acts.shape[0]
    k_in = proj_in.shape[1]
    nblk, blk, k_out = block_vals.shape
    feat = k_in * k_out
    nb = feat // FB // mp
    need = max(16, k_in // mp)
    vmem = pl.BlockSpec(memory_space=pltpu.VMEM)
    hbm = pl.BlockSpec(memory_space=pltpu.HBM)
    local = grads.shape[1] // blk
    ids = lax.axis_index("mp") * local + jnp.arange(local, dtype=jnp.int32)
    order = jnp.arange(nblk, dtype=jnp.int32)
    inverse = jnp.min(jnp.where(block_index[None, :] == ids[:, None], order[None, :], nblk), axis=1)
    full, gath = pl.pallas_call(
        functools.partial(coords_kernel, mp, dp, need),
        out_shape=(jax.ShapeDtypeStruct((k_in + k_out, ex), BF16),
                   jax.ShapeDtypeStruct((dp, need + k_out, ex), BF16)),
        in_specs=[pl.BlockSpec(memory_space=pltpu.SMEM), vmem] + [hbm] * 4,
        out_specs=(vmem, vmem),
        scratch_shapes=[
            pltpu.VMEM(acts.shape, BF16),
            pltpu.VMEM(grads.shape, BF16),
            pltpu.VMEM((k_in, acts.shape[1]), BF16),
            pltpu.VMEM((nblk + 1, k_out, blk), BF16),
            pltpu.VMEM((k_out, grads.shape[1]), BF16),
            pltpu.VMEM((k_in + k_out, ex), BF16),
            pltpu.VMEM((mp, k_in + k_out, ex), BF16),
            pltpu.VMEM((need + k_out, ex), BF16),
            pltpu.SemaphoreType.DMA((4,)),
            pltpu.SemaphoreType.DMA((2, mp - 1)),
            pltpu.SemaphoreType.DMA((2, mp - 1)),
            pltpu.SemaphoreType.DMA((dp - 1,)),
            pltpu.SemaphoreType.DMA((dp - 1,)),
        ],
        compiler_params=pltpu.CompilerParams(
            collective_id=0, has_side_effects=True, vmem_limit_bytes=63 << 20),
    )(inverse, assign, acts, grads, proj_in.T, jnp.swapaxes(block_vals, 1, 2))
    features, factor = pl.pallas_call(
        functools.partial(factor_kernel, mp, k_in, k_out, need),
        out_shape=(jax.ShapeDtypeStruct((ex // mp, feat), BF16),
                   jax.ShapeDtypeStruct((nb, FB, FB), F32)),
        in_specs=[hbm, hbm],
        out_specs=(hbm, hbm),
        scratch_shapes=[
            pltpu.VMEM(gath.shape, BF16),
            pltpu.VMEM(full.shape, BF16),
            pltpu.VMEM((ex // mp, feat), BF16),
            pltpu.VMEM((nb, FB, FB), F32),
            pltpu.VMEM((nb * FB, dp * ex), BF16),
            pltpu.VMEM((need, ex), F32),
            pltpu.VMEM((nb, FB, FB), F32),
            pltpu.VMEM((nb, FB // TILE, TILE, TILE), F32),
            pltpu.VMEM((nb, FB // TILE, TILE, TILE), F32),
            pltpu.SemaphoreType.DMA((2,)),
            pltpu.SemaphoreType.DMA(()),
            pltpu.SemaphoreType.DMA((nb, FB // TILE)),
        ],
        compiler_params=pltpu.CompilerParams(vmem_limit_bytes=48 << 20),
    )(gath, full)
    return features, factor


def solution(mesh):
    return jax.shard_map(
        shards,
        mesh=mesh,
        in_specs=(P("dp", "mp"), P("dp", "mp"), P(), P(), P(), P("dp", None)),
        out_specs=(P(("dp", "mp"), None), P("mp", None, None)),
        check_vma=False,
    )
```

```python
import functools

import jax
import jax.numpy as jnp
from jax import lax
from jax.experimental import pallas as pl
from jax.experimental.pallas import tpu as pltpu
from jax.sharding import PartitionSpec as P

MESH = pl.DeviceIdType.MESH
FB = 512
DAMPING = 0.05
TILE = 128
STEP = 16
F32 = jnp.float32
BF16 = jnp.bfloat16


def dot_nt(a, b):
    return lax.dot_general(a, b, (((1,), (1,)), ((), ())), preferred_element_type=F32)


def dot_tn(a, b):
    return lax.dot_general(a, b, (((0,), (0,)), ((), ())), preferred_element_type=F32)


def coords_kernel(mp, dp, need, inverse_ref, assign_ref, acts_hbm, grads_hbm, proj_hbm, vals_hbm, full_ref, gath_ref,
                  acts, grads, proj, vals, dense, part, recv, slab, ins, s1, r1, s2, r2):
    m = lax.axis_index("mp")
    d = lax.axis_index("dp")
    barrier = pltpu.get_barrier_semaphore()
    for o in range(1, mp):
        pl.semaphore_signal(barrier, inc=1, device_id=(d, lax.rem(m + o, mp)), device_id_type=MESH)
    for o in range(1, dp):
        pl.semaphore_signal(barrier, inc=1, device_id=(lax.rem(d + o, dp), m), device_id_type=MESH)
    ex, width = acts.shape
    k_in = proj.shape[0]
    nblk, k_out, blk = vals_hbm.shape
    local = grads.shape[1] // blk
    cols = pl.ds(pl.multiple_of(m * width, width), width)
    loads = [
        pltpu.make_async_copy(proj_hbm.at[:, cols], proj, ins.at[0]),
        pltpu.make_async_copy(acts_hbm, acts, ins.at[1]),
        pltpu.make_async_copy(vals_hbm, vals.at[pl.ds(0, nblk)], ins.at[2]),
        pltpu.make_async_copy(grads_hbm, grads, ins.at[3]),
    ]
    for load in loads:
        load.start()
    vals[nblk] = jnp.zeros((k_out, blk), BF16)
    pick = (lax.broadcasted_iota(jnp.int32, (ex, ex), 0) == assign_ref[...]).astype(BF16)

    def send(lo, hi, at):
        copies = []
        for o in range(1, mp):
            copy = pltpu.make_async_remote_copy(
                src_ref=part.at[pl.ds(lo, hi - lo)], dst_ref=recv.at[m, pl.ds(lo, hi - lo)],
                send_sem=s1.at[at, o - 1], recv_sem=r1.at[at, o - 1],
                device_id=(d, lax.rem(m + o, mp)), device_id_type=MESH)
            copy.start()
            copies.append(copy)
        recv[m, lo:hi] = part[lo:hi]
        return copies

    loads[0].wait()
    loads[1].wait()
    in_part = dot_nt(proj[...], acts[...])
    part[:k_in] = jnp.dot(in_part.astype(BF16), pick, preferred_element_type=F32).astype(BF16)
    pl.semaphore_wait(barrier, mp + dp - 2)
    in_copies = send(0, k_in, 0)
    loads[2].wait()
    for b in range(local):
        dense[:, b * blk:(b + 1) * blk] = vals[inverse_ref[b]]
    loads[3].wait()
    out_part = dot_nt(dense[...], grads[...])
    part[k_in:] = jnp.dot(out_part.astype(BF16), pick, preferred_element_type=F32).astype(BF16)
    out_copies = send(k_in, k_in + k_out, 1)

    def add_up(lo, hi):
        total = recv[0, lo:hi].astype(F32)
        for j in range(1, mp):
            total = total + recv[j, lo:hi].astype(F32)
        return total.astype(BF16)

    for copy in in_copies:
        copy.wait()
    full_ref[:k_in] = add_up(0, k_in)
    first = (m * (k_in // mp)) // need * need
    slab[:need] = full_ref[pl.ds(pl.multiple_of(first, need), need), :]
    for copy in out_copies:
        copy.wait()
    slab[need:] = add_up(k_in, k_in + k_out)
    copies = []
    for o in range(1, dp):
        copy = pltpu.make_async_remote_copy(
            src_ref=slab, dst_ref=gath_ref.at[d], send_sem=s2.at[o - 1], recv_sem=r2.at[o - 1],
            device_id=(lax.rem(d + o, dp), m), device_id_type=MESH)
        copy.start()
        copies.append(copy)
    full_ref[k_in:] = slab[need:]
    gath_ref[d] = slab[...]
    for copy in copies:
        copy.wait()


def split(x):
    high = x.astype(BF16).astype(F32)
    return high, x - high


def eliminate(heads, tails, rows):
    half = STEP // 2
    sub = lax.broadcasted_iota(jnp.int32, (half, TILE), 0)
    scale = [jnp.zeros((half, TILE), F32) for _ in range(2)]
    tops = [row[:half] for row in rows]
    ends = [row[half:] for row in rows]

    def spread(x, at):
        return jnp.broadcast_to(x[at:at + 1, :], (half, TILE))

    def reduce_rows(low, at, top, end):
        if low:
            top = jnp.where(sub > at, top, 0.0)
        else:
            end = jnp.where(sub > at, end, 0.0)
        for t in range(len(rows)):
            row = spread(tops[t] if low else ends[t], at)
            if low and at < half - 1:
                tops[t] = tops[t] - top * row
            ends[t] = ends[t] - end * row

    for k in range(0, STEP, 2):
        low, at = k < half, k % half
        x, y = (heads[k], heads[k + 1]) if low else (tails[k], tails[k + 1])
        p, e, q = spread(x, at), spread(x, at + 1), spread(y, at + 1)
        det = p * q - e * e
        root_p, root_d = lax.rsqrt(p), lax.rsqrt(det)
        inv_p = root_p * root_p
        inv_s = (root_d * root_d) * p
        ratio = e * inv_p
        scale[k // half] = jnp.where(sub == at, root_p, scale[k // half])
        scale[k // half] = jnp.where(sub == at + 1, root_d * (p * root_p), scale[k // half])
        end_x = tails[k] * inv_p
        tails[k + 1] = tails[k + 1] - tails[k] * ratio
        end_y = tails[k + 1] * inv_s
        top_x = top_y = None
        if low:
            top_x = heads[k] * inv_p
            heads[k + 1] = heads[k + 1] - heads[k] * ratio
            top_y = heads[k + 1] * inv_s
        for j in range(k + 2, STEP):
            if j < half:
                xj, yj = spread(heads[k], j), spread(heads[k + 1], j)
                heads[j] = (heads[j] - top_x * xj) - top_y * yj
            else:
                xj, yj = spread(tails[k], j - half), spread(tails[k + 1], j - half)
            tails[j] = (tails[j] - end_x * xj) - end_y * yj
        reduce_rows(low, at, top_x, end_x)
        if k + 1 < STEP - 1:
            reduce_rows(low, at + 1, top_y, end_y)
    return [jnp.concatenate([top * scale[0], end * scale[1]], axis=0) for top, end in zip(tops, ends)]


def factor_kernel(mp, k_in, k_out, need, gath_hbm, full_hbm, feat_hbm, factor_hbm,
                  gath_ref, full_ref, feat_ref, factor_ref, ft, inf, cov, panel, upper, left, right, ins, fsem, osem):
    m = lax.axis_index("mp")
    dp, _, ex = gath_ref.shape
    nb = factor_ref.shape[0]
    tiles = FB // TILE
    per = FB // k_out
    skip = m * (k_in // mp) - (m * (k_in // mp)) // need * need

    full_load = pltpu.make_async_copy(full_hbm, full_ref, ins.at[0])
    gath_load = pltpu.make_async_copy(gath_hbm, gath_ref, ins.at[1])
    full_load.start()
    gath_load.start()
    full_load.wait()

    mine = feat_ref.shape[0]
    pick = (lax.broadcasted_iota(jnp.int32, (mine, ex), 0) + m * mine
            == lax.broadcasted_iota(jnp.int32, (mine, ex), 1)).astype(BF16)
    coords = dot_nt(pick, full_ref[...])
    lane = lax.broadcasted_iota(jnp.int32, (mine, TILE), 1)
    outs = jnp.concatenate([coords[:, k_in:], coords[:, k_in:]], axis=1)
    for t in range(k_in // 2):
        even = jnp.broadcast_to(coords[:, 2 * t:2 * t + 1], (mine, TILE))
        odd = jnp.broadcast_to(coords[:, 2 * t + 1:2 * t + 2], (mine, TILE))
        feat_ref[:, t * TILE:(t + 1) * TILE] = (jnp.where(lane < k_out, even, odd) * outs).astype(BF16)

    feat_store = pltpu.make_async_copy(feat_ref, feat_hbm, fsem)
    feat_store.start()
    gath_load.wait()

    def expand(g, carry):
        inf[...] = gath_ref[g, :need, :].astype(F32)
        out = gath_ref[g, need:, :].astype(F32)
        at = pl.ds(pl.multiple_of(g * ex, ex), ex)
        for p in range(nb * per):
            if nb * per == need:
                row = inf[p:p + 1, :]
            else:
                row = inf[pl.ds(skip + p, 1), :]
            ft[p * k_out:(p + 1) * k_out, at] = (row * out).astype(BF16)
        return carry

    lax.fori_loop(0, dp, expand, 0)

    total = dp * ex
    chunk = min(total, 1024)
    half = FB // 2
    diag = jnp.where(lax.broadcasted_iota(jnp.int32, (half, half), 0)
                     == lax.broadcasted_iota(jnp.int32, (half, half), 1), DAMPING, 0.0)
    for c in range(nb):
        for i in range(2):
            for j in range(i, 2):
                def piece(n):
                    at = pl.ds(pl.multiple_of(n * chunk, chunk), chunk)
                    return dot_nt(ft[c * FB + i * half:c * FB + (i + 1) * half, at],
                                  ft[c * FB + j * half:c * FB + (j + 1) * half, at])
                gram = piece(0)
                if total > chunk:
                    gram = lax.fori_loop(1, total // chunk, lambda n, acc: acc + piece(n), gram)
                gram = gram * (1.0 / total)
                if i == j:
                    gram = gram + diag
                cov[c, i * half:(i + 1) * half, j * half:(j + 1) * half] = gram

    def block_row(b, carry):
        at = pl.ds(pl.multiple_of(b * TILE, TILE), TILE)

        def tile_at(t):
            return pl.ds(pl.multiple_of(lax.rem(b + t, tiles) * TILE, TILE), TILE)

        for c in range(nb):
            for t in range(tiles):
                panel[c, t] = cov[c, at, tile_at(t)]
        for s in range(TILE // STEP):
            lo, hi = s * STEP, (s + 1) * STEP
            cols = []
            for c in range(nb):
                pivot = panel[c, 0, lo:hi, :]
                half = STEP // 2
                cols.append((
                    [jnp.broadcast_to(pivot[:half, lo + j:lo + j + 1], (half, TILE)) for j in range(half)],
                    [jnp.broadcast_to(pivot[half:, lo + j:lo + j + 1], (half, TILE)) for j in range(STEP)]))
            for c in range(nb):
                rows = eliminate(*cols[c], [panel[c, t, lo:hi, :] for t in range(tiles)])
                parts = [split(row) for row in rows]
                for t in range(tiles):
                    upper[c, t, lo:hi, :] = rows[t]
                if hi < TILE:
                    h, l = parts[0]
                    lhs = jnp.concatenate([h, h, l, l], axis=0)[:, hi:].astype(BF16)
                    rhs = jnp.concatenate(
                        [jnp.concatenate([h, l, h, l], axis=0) for h, l in parts], axis=1).astype(BF16)
                    update = dot_tn(lhs, rhs)
                    for t in range(tiles):
                        panel[c, t, hi:, :] = panel[c, t, hi:, :] - update[:, t * TILE:(t + 1) * TILE]
        tri = (lax.broadcasted_iota(jnp.int32, (TILE, TILE), 1)
               >= lax.broadcasted_iota(jnp.int32, (TILE, TILE), 0))
        for c in range(nb):
            factor_ref[c, at, tile_at(0)] = jnp.where(tri, upper[c, 0], 0.0)
            for t in range(1, tiles):
                factor_ref[c, at, tile_at(t)] = jnp.where(b + t < tiles, upper[c, t], 0.0)
            pltpu.make_async_copy(factor_ref.at[c, at], factor_hbm.at[c, at], osem.at[c, b]).start()
        @pl.when(b < tiles - 1)
        def _():
            for c in range(nb):
                for t in range(tiles):
                    h, l = split(upper[c, t])
                    h, l = h.astype(BF16), l.astype(BF16)
                    for n, (a, z) in enumerate(((h, h), (h, l), (l, h), (l, l))):
                        left[c, n * TILE:(n + 1) * TILE, t * TILE:(t + 1) * TILE] = a
                        right[c, n * TILE:(n + 1) * TILE, t * TILE:(t + 1) * TILE] = z

        for i in range(1, tiles):
            @pl.when(b + i < tiles)
            def _():
                here = pl.ds(pl.multiple_of(lax.rem(b + i, tiles) * TILE, TILE), TILE)
                for c in range(nb):
                    update = dot_tn(left[c, :, i * TILE:(i + 1) * TILE], right[c, :, i * TILE:])
                    for t in range(i, tiles):
                        cov[c, here, tile_at(t)] = cov[c, here, tile_at(t)] - update[:, (t - i) * TILE:(t - i + 1) * TILE]
        return carry

    lax.fori_loop(0, tiles, block_row, 0)
    feat_store.wait()
    for c in range(nb):
        for b in range(tiles):
            at = pl.ds(b * TILE, TILE)
            pltpu.make_async_copy(factor_ref.at[c, at], factor_hbm.at[c, at], osem.at[c, b]).wait()


def shards(acts, grads, proj_in, block_vals, block_index, assign):
    mp = lax.axis_size("mp")
    dp = lax.axis_size("dp")
    ex = acts.shape[0]
    k_in = proj_in.shape[1]
    nblk, blk, k_out = block_vals.shape
    feat = k_in * k_out
    nb = feat // FB // mp
    need = max(16, k_in // mp)
    vmem = pl.BlockSpec(memory_space=pltpu.VMEM)
    hbm = pl.BlockSpec(memory_space=pltpu.HBM)
    local = grads.shape[1] // blk
    ids = lax.axis_index("mp") * local + jnp.arange(local, dtype=jnp.int32)
    order = jnp.arange(nblk, dtype=jnp.int32)
    inverse = jnp.min(jnp.where(block_index[None, :] == ids[:, None], order[None, :], nblk), axis=1)
    full, gath = pl.pallas_call(
        functools.partial(coords_kernel, mp, dp, need),
        out_shape=(jax.ShapeDtypeStruct((k_in + k_out, ex), BF16),
                   jax.ShapeDtypeStruct((dp, need + k_out, ex), BF16)),
        in_specs=[pl.BlockSpec(memory_space=pltpu.SMEM), vmem] + [hbm] * 4,
        out_specs=(vmem, vmem),
        scratch_shapes=[
            pltpu.VMEM(acts.shape, BF16),
            pltpu.VMEM(grads.shape, BF16),
            pltpu.VMEM((k_in, acts.shape[1]), BF16),
            pltpu.VMEM((nblk + 1, k_out, blk), BF16),
            pltpu.VMEM((k_out, grads.shape[1]), BF16),
            pltpu.VMEM((k_in + k_out, ex), BF16),
            pltpu.VMEM((mp, k_in + k_out, ex), BF16),
            pltpu.VMEM((need + k_out, ex), BF16),
            pltpu.SemaphoreType.DMA((4,)),
            pltpu.SemaphoreType.DMA((2, mp - 1)),
            pltpu.SemaphoreType.DMA((2, mp - 1)),
            pltpu.SemaphoreType.DMA((dp - 1,)),
            pltpu.SemaphoreType.DMA((dp - 1,)),
        ],
        compiler_params=pltpu.CompilerParams(
            collective_id=0, has_side_effects=True, vmem_limit_bytes=63 << 20),
    )(inverse, assign, acts, grads, proj_in.T, jnp.swapaxes(block_vals, 1, 2))
    features, factor = pl.pallas_call(
        functools.partial(factor_kernel, mp, k_in, k_out, need),
        out_shape=(jax.ShapeDtypeStruct((ex // mp, feat), BF16),
                   jax.ShapeDtypeStruct((nb, FB, FB), F32)),
        in_specs=[hbm, hbm],
        out_specs=(hbm, hbm),
        scratch_shapes=[
            pltpu.VMEM(gath.shape, BF16),
            pltpu.VMEM(full.shape, BF16),
            pltpu.VMEM((ex // mp, feat), BF16),
            pltpu.VMEM((nb, FB, FB), F32),
            pltpu.VMEM((nb * FB, dp * ex), BF16),
            pltpu.VMEM((need, ex), F32),
            pltpu.VMEM((nb, FB, FB), F32),
            pltpu.VMEM((nb, FB // TILE, TILE, TILE), F32),
            pltpu.VMEM((nb, FB // TILE, TILE, TILE), F32),
            pltpu.VMEM((nb, 4 * TILE, FB), BF16),
            pltpu.VMEM((nb, 4 * TILE, FB), BF16),
            pltpu.SemaphoreType.DMA((2,)),
            pltpu.SemaphoreType.DMA(()),
            pltpu.SemaphoreType.DMA((nb, FB // TILE)),
        ],
        compiler_params=pltpu.CompilerParams(vmem_limit_bytes=63 << 20),
    )(gath, full)
    return features, factor


def solution(mesh):
    return jax.shard_map(
        shards,
        mesh=mesh,
        in_specs=(P("dp", "mp"), P("dp", "mp"), P(), P(), P(), P("dp", None)),
        out_specs=(P(("dp", "mp"), None), P("mp", None, None)),
        check_vma=False,
    )
```

```python
import functools

import jax
import jax.numpy as jnp
from jax import lax
from jax.experimental import pallas as pl
from jax.experimental.pallas import tpu as pltpu
from jax.sharding import PartitionSpec as P

MESH = pl.DeviceIdType.MESH
FB = 512
DAMPING = 0.05
TILE = 128
STEP = 16
F32 = jnp.float32
BF16 = jnp.bfloat16


def dot_nt(a, b):
    return lax.dot_general(a, b, (((1,), (1,)), ((), ())), preferred_element_type=F32)


def dot_tn(a, b):
    return lax.dot_general(a, b, (((0,), (0,)), ((), ())), preferred_element_type=F32)


def coords_kernel(mp, dp, need, inverse_ref, assign_ref, acts_hbm, grads_hbm, proj_hbm, vals_hbm, full_ref, gath_ref,
                  acts, grads, proj, vals, dense, part, recv, slab, ins, s1, r1, s2, r2):
    m = lax.axis_index("mp")
    d = lax.axis_index("dp")
    barrier = pltpu.get_barrier_semaphore()
    for o in range(1, mp):
        pl.semaphore_signal(barrier, inc=1, device_id=(d, lax.rem(m + o, mp)), device_id_type=MESH)
    for o in range(1, dp):
        pl.semaphore_signal(barrier, inc=1, device_id=(lax.rem(d + o, dp), m), device_id_type=MESH)
    ex, width = acts.shape
    k_in = proj.shape[0]
    nblk, k_out, blk = vals_hbm.shape
    local = grads.shape[1] // blk
    cols = pl.ds(pl.multiple_of(m * width, width), width)
    loads = [
        pltpu.make_async_copy(proj_hbm.at[:, cols], proj, ins.at[0]),
        pltpu.make_async_copy(acts_hbm, acts, ins.at[1]),
        pltpu.make_async_copy(vals_hbm, vals.at[pl.ds(0, nblk)], ins.at[2]),
        pltpu.make_async_copy(grads_hbm, grads, ins.at[3]),
    ]
    for load in loads:
        load.start()
    vals[nblk] = jnp.zeros((k_out, blk), BF16)
    pick = (lax.broadcasted_iota(jnp.int32, (ex, ex), 0) == assign_ref[...]).astype(BF16)

    def send(lo, hi, at):
        copies = []
        for o in range(1, mp):
            copy = pltpu.make_async_remote_copy(
                src_ref=part.at[pl.ds(lo, hi - lo)], dst_ref=recv.at[m, pl.ds(lo, hi - lo)],
                send_sem=s1.at[at, o - 1], recv_sem=r1.at[at, o - 1],
                device_id=(d, lax.rem(m + o, mp)), device_id_type=MESH)
            copy.start()
            copies.append(copy)
        recv[m, lo:hi] = part[lo:hi]
        return copies

    loads[0].wait()
    loads[1].wait()
    in_part = dot_nt(proj[...], acts[...])
    part[:k_in] = jnp.dot(in_part.astype(BF16), pick, preferred_element_type=F32).astype(BF16)
    pl.semaphore_wait(barrier, mp + dp - 2)
    in_copies = send(0, k_in, 0)
    loads[2].wait()
    for b in range(local):
        dense[:, b * blk:(b + 1) * blk] = vals[inverse_ref[b]]
    loads[3].wait()
    out_part = dot_nt(dense[...], grads[...])
    part[k_in:] = jnp.dot(out_part.astype(BF16), pick, preferred_element_type=F32).astype(BF16)
    out_copies = send(k_in, k_in + k_out, 1)

    def add_up(lo, hi):
        total = recv[0, lo:hi].astype(F32)
        for j in range(1, mp):
            total = total + recv[j, lo:hi].astype(F32)
        return total.astype(BF16)

    for copy in in_copies:
        copy.wait()
    full_ref[:k_in] = add_up(0, k_in)
    first = (m * (k_in // mp)) // need * need
    slab[:need] = full_ref[pl.ds(pl.multiple_of(first, need), need), :]
    for copy in out_copies:
        copy.wait()
    slab[need:] = add_up(k_in, k_in + k_out)
    copies = []
    for o in range(1, dp):
        copy = pltpu.make_async_remote_copy(
            src_ref=slab, dst_ref=gath_ref.at[d], send_sem=s2.at[o - 1], recv_sem=r2.at[o - 1],
            device_id=(lax.rem(d + o, dp), m), device_id_type=MESH)
        copy.start()
        copies.append(copy)
    full_ref[k_in:] = slab[need:]
    gath_ref[d] = slab[...]
    for copy in copies:
        copy.wait()


def eliminate(heads, tails, rows):
    half = STEP // 2
    sub = lax.broadcasted_iota(jnp.int32, (half, TILE), 0)
    scale = [jnp.zeros((half, TILE), F32) for _ in range(2)]
    tops = [row[:half] for row in rows]
    ends = [row[half:] for row in rows]

    def spread(x, at):
        return jnp.broadcast_to(x[at:at + 1, :], (half, TILE))

    def reduce_rows(low, at, top, end):
        if low:
            top = jnp.where(sub > at, top, 0.0)
        else:
            end = jnp.where(sub > at, end, 0.0)
        for t in range(len(rows)):
            row = spread(tops[t] if low else ends[t], at)
            if low and at < half - 1:
                tops[t] = tops[t] - top * row
            ends[t] = ends[t] - end * row

    for k in range(0, STEP, 2):
        low, at = k < half, k % half
        x, y = (heads[k], heads[k + 1]) if low else (tails[k], tails[k + 1])
        p, e, q = spread(x, at), spread(x, at + 1), spread(y, at + 1)
        det = p * q - e * e
        root_p, root_d = lax.rsqrt(p), lax.rsqrt(det)
        inv_p = root_p * root_p
        inv_s = (root_d * root_d) * p
        ratio = e * inv_p
        scale[k // half] = jnp.where(sub == at, root_p, scale[k // half])
        scale[k // half] = jnp.where(sub == at + 1, root_d * (p * root_p), scale[k // half])
        end_x = tails[k] * inv_p
        tails[k + 1] = tails[k + 1] - tails[k] * ratio
        end_y = tails[k + 1] * inv_s
        top_x = top_y = None
        if low:
            top_x = heads[k] * inv_p
            heads[k + 1] = heads[k + 1] - heads[k] * ratio
            top_y = heads[k + 1] * inv_s
        for j in range(k + 2, STEP):
            if j < half:
                xj, yj = spread(heads[k], j), spread(heads[k + 1], j)
                heads[j] = (heads[j] - top_x * xj) - top_y * yj
            else:
                xj, yj = spread(tails[k], j - half), spread(tails[k + 1], j - half)
            tails[j] = (tails[j] - end_x * xj) - end_y * yj
        reduce_rows(low, at, top_x, end_x)
        if k + 1 < STEP - 1:
            reduce_rows(low, at + 1, top_y, end_y)
    return [jnp.concatenate([top * scale[0], end * scale[1]], axis=0) for top, end in zip(tops, ends)]


def factor_kernel(mp, k_in, k_out, need, gath_hbm, full_hbm, feat_hbm, factor_hbm,
                  gath_ref, full_ref, feat_ref, factor_ref, ft, inf, cov, left, right, ins, fsem, osem):
    m = lax.axis_index("mp")
    dp, _, ex = gath_ref.shape
    nb = factor_ref.shape[0]
    tiles = FB // TILE
    per = FB // k_out
    skip = m * (k_in // mp) - (m * (k_in // mp)) // need * need

    full_load = pltpu.make_async_copy(full_hbm, full_ref, ins.at[0])
    gath_load = pltpu.make_async_copy(gath_hbm, gath_ref, ins.at[1])
    full_load.start()
    gath_load.start()
    full_load.wait()

    mine = feat_ref.shape[0]
    pick = (lax.broadcasted_iota(jnp.int32, (mine, ex), 0) + m * mine
            == lax.broadcasted_iota(jnp.int32, (mine, ex), 1)).astype(BF16)
    coords = dot_nt(pick, full_ref[...])
    lane = lax.broadcasted_iota(jnp.int32, (mine, TILE), 1)
    outs = jnp.concatenate([coords[:, k_in:], coords[:, k_in:]], axis=1)
    for t in range(k_in // 2):
        even = jnp.broadcast_to(coords[:, 2 * t:2 * t + 1], (mine, TILE))
        odd = jnp.broadcast_to(coords[:, 2 * t + 1:2 * t + 2], (mine, TILE))
        feat_ref[:, t * TILE:(t + 1) * TILE] = (jnp.where(lane < k_out, even, odd) * outs).astype(BF16)

    feat_store = pltpu.make_async_copy(feat_ref, feat_hbm, fsem)
    feat_store.start()
    gath_load.wait()

    def expand(g, carry):
        inf[...] = gath_ref[g, :need, :].astype(F32)
        out = gath_ref[g, need:, :].astype(F32)
        at = pl.ds(pl.multiple_of(g * ex, ex), ex)
        for p in range(nb * per):
            if nb * per == need:
                row = inf[p:p + 1, :]
            else:
                row = inf[pl.ds(skip + p, 1), :]
            ft[p * k_out:(p + 1) * k_out, at] = (row * out).astype(BF16)
        return carry

    lax.fori_loop(0, dp, expand, 0)

    total = dp * ex
    chunk = min(total, 1024)
    mid = FB // 2
    diag = jnp.where(lax.broadcasted_iota(jnp.int32, (mid, mid), 0)
                     == lax.broadcasted_iota(jnp.int32, (mid, mid), 1), DAMPING, 0.0)
    for c in range(nb):
        for i in range(2):
            for j in range(i, 2):
                def piece(n):
                    at = pl.ds(pl.multiple_of(n * chunk, chunk), chunk)
                    return dot_nt(ft[c * FB + i * mid:c * FB + (i + 1) * mid, at],
                                  ft[c * FB + j * mid:c * FB + (j + 1) * mid, at])
                gram = piece(0)
                if total > chunk:
                    gram = lax.fori_loop(1, total // chunk, lambda n, acc: acc + piece(n), gram)
                gram = gram * (1.0 / total)
                if i == j:
                    gram = gram + diag
                cov[c, i * mid:(i + 1) * mid, j * mid:(j + 1) * mid] = gram

    tri = (lax.broadcasted_iota(jnp.int32, (TILE, TILE), 1)
           >= lax.broadcasted_iota(jnp.int32, (TILE, TILE), 0))
    half = STEP // 2
    stores = []
    for b in range(tiles):
        lead, count = b * TILE, tiles - b
        for c in range(nb):
            if b:
                factor_ref[c, lead:lead + TILE, :lead] = jnp.zeros((TILE, lead), F32)
        for s in range(TILE // STEP):
            lo, hi = lead + s * STEP, lead + (s + 1) * STEP
            at = s * STEP
            cols = []
            for c in range(nb):
                pivot = cov[c, lo:hi, lead:lead + TILE]
                cols.append((
                    [jnp.broadcast_to(pivot[:half, at + j:at + j + 1], (half, TILE)) for j in range(half)],
                    [jnp.broadcast_to(pivot[half:, at + j:at + j + 1], (half, TILE)) for j in range(STEP)]))
            for c in range(nb):
                rows = eliminate(*cols[c], [cov[c, lo:hi, lead + t * TILE:lead + (t + 1) * TILE] for t in range(count)])
                high = [row.astype(BF16) for row in rows]
                low = [(row - h.astype(F32)).astype(BF16) for row, h in zip(rows, high)]
                for t in range(count):
                    row = rows[t]
                    if t == 0:
                        row = jnp.where(tri[at:at + STEP], row, 0.0)
                    factor_ref[c, lo:hi, lead + t * TILE:lead + (t + 1) * TILE] = row
                if hi < lead + TILE:
                    lhs = jnp.concatenate([high[0], high[0], low[0], low[0]], axis=0)[:, at + STEP:]
                    rhs = jnp.concatenate(
                        [jnp.concatenate([h, l, h, l], axis=0) for h, l in zip(high, low)], axis=1)
                    cov[c, hi:lead + TILE, lead:] = cov[c, hi:lead + TILE, lead:] - dot_tn(lhs, rhs)
                if count > 1:
                    for t in range(1, count):
                        for n in range(4):
                            to = slice(n * TILE + at, n * TILE + at + STEP)
                            left[c, to, t * TILE:(t + 1) * TILE] = (high if n < 2 else low)[t]
                            right[c, to, t * TILE:(t + 1) * TILE] = (low if n % 2 else high)[t]
        for c in range(nb):
            store = pltpu.make_async_copy(
                factor_ref.at[c, pl.ds(lead, TILE)], factor_hbm.at[c, pl.ds(lead, TILE)], osem.at[c, b])
            store.start()
            stores.append(store)
        for i in range(1, count):
            here = lead + i * TILE
            for c in range(nb):
                update = dot_tn(left[c, :, i * TILE:(i + 1) * TILE], right[c, :, i * TILE:count * TILE])
                cov[c, here:here + TILE, here:] = cov[c, here:here + TILE, here:] - update
    for store in stores:
        store.wait()
    feat_store.wait()


def shards(acts, grads, proj_in, block_vals, block_index, assign):
    mp = lax.axis_size("mp")
    dp = lax.axis_size("dp")
    ex = acts.shape[0]
    k_in = proj_in.shape[1]
    nblk, blk, k_out = block_vals.shape
    feat = k_in * k_out
    nb = feat // FB // mp
    need = max(16, k_in // mp)
    vmem = pl.BlockSpec(memory_space=pltpu.VMEM)
    hbm = pl.BlockSpec(memory_space=pltpu.HBM)
    local = grads.shape[1] // blk
    ids = lax.axis_index("mp") * local + jnp.arange(local, dtype=jnp.int32)
    order = jnp.arange(nblk, dtype=jnp.int32)
    inverse = jnp.min(jnp.where(block_index[None, :] == ids[:, None], order[None, :], nblk), axis=1)
    full, gath = pl.pallas_call(
        functools.partial(coords_kernel, mp, dp, need),
        out_shape=(jax.ShapeDtypeStruct((k_in + k_out, ex), BF16),
                   jax.ShapeDtypeStruct((dp, need + k_out, ex), BF16)),
        in_specs=[pl.BlockSpec(memory_space=pltpu.SMEM), vmem] + [hbm] * 4,
        out_specs=(vmem, vmem),
        scratch_shapes=[
            pltpu.VMEM(acts.shape, BF16),
            pltpu.VMEM(grads.shape, BF16),
            pltpu.VMEM((k_in, acts.shape[1]), BF16),
            pltpu.VMEM((nblk + 1, k_out, blk), BF16),
            pltpu.VMEM((k_out, grads.shape[1]), BF16),
            pltpu.VMEM((k_in + k_out, ex), BF16),
            pltpu.VMEM((mp, k_in + k_out, ex), BF16),
            pltpu.VMEM((need + k_out, ex), BF16),
            pltpu.SemaphoreType.DMA((4,)),
            pltpu.SemaphoreType.DMA((2, mp - 1)),
            pltpu.SemaphoreType.DMA((2, mp - 1)),
            pltpu.SemaphoreType.DMA((dp - 1,)),
            pltpu.SemaphoreType.DMA((dp - 1,)),
        ],
        compiler_params=pltpu.CompilerParams(
            collective_id=0, has_side_effects=True, vmem_limit_bytes=63 << 20),
    )(inverse, assign, acts, grads, proj_in.T, jnp.swapaxes(block_vals, 1, 2))
    features, factor = pl.pallas_call(
        functools.partial(factor_kernel, mp, k_in, k_out, need),
        out_shape=(jax.ShapeDtypeStruct((ex // mp, feat), BF16),
                   jax.ShapeDtypeStruct((nb, FB, FB), F32)),
        in_specs=[hbm, hbm],
        out_specs=(hbm, hbm),
        scratch_shapes=[
            pltpu.VMEM(gath.shape, BF16),
            pltpu.VMEM(full.shape, BF16),
            pltpu.VMEM((ex // mp, feat), BF16),
            pltpu.VMEM((nb, FB, FB), F32),
            pltpu.VMEM((nb * FB, dp * ex), BF16),
            pltpu.VMEM((need, ex), F32),
            pltpu.VMEM((nb, FB, FB), F32),
            pltpu.VMEM((nb, 4 * TILE, FB), BF16),
            pltpu.VMEM((nb, 4 * TILE, FB), BF16),
            pltpu.SemaphoreType.DMA((2,)),
            pltpu.SemaphoreType.DMA(()),
            pltpu.SemaphoreType.DMA((nb, FB // TILE)),
        ],
        compiler_params=pltpu.CompilerParams(vmem_limit_bytes=63 << 20),
    )(gath, full)
    return features, factor


def solution(mesh):
    return jax.shard_map(
        shards,
        mesh=mesh,
        in_specs=(P("dp", "mp"), P("dp", "mp"), P(), P(), P(), P("dp", None)),
        out_specs=(P(("dp", "mp"), None), P("mp", None, None)),
        check_vma=False,
    )
```
